32 devices in a mesh: island: 4 (over y, core), fsdp: 8 (over z, x).
Axes of the slice: x: 2, y: 2, z: 4, core: 2. Of those that a mesh axis runs over, the one named last changes fastest.
Arguments:
- params: float32 [4, 128, 2, 6656], P('island', 'fsdp'), may hold values from -40 to 40
- adam_m: float32 [4, 128, 2, 6656], P('island', 'fsdp'), may hold values from -3 to 3
- adam_v: float32 [4, 128, 2, 6656], P('island', 'fsdp'), may hold values from 0.1 to 4
- outer_params: float32 [128, 2, 6656], P('fsdp'), may hold values from -6 to 6
- outer_mom: float32 [128, 2, 6656], P('fsdp'), may hold values from -3 to 3
- obs_ids: int32 [4, 4096], P('island', 'fsdp'), may hold values from 0 to 127
- act_ids: int32 [4, 4096], P('island', 'fsdp'), may hold values from 0 to 127
- fragment: int32 [1], replicated, may hold values from 0 to 51
Outputs:
- new_params: float32 [4, 128, 2, 6656], P('island', 'fsdp')
- new_moment: float32 [4, 128, 2, 6656], P('island', 'fsdp')
- new_second: float32 [4, 128, 2, 6656], P('island', 'fsdp')
- new_outer: float32 [128, 2, 6656], P('fsdp')
- new_outer_mom: float32 [128, 2, 6656], P('fsdp')
The draws below stay inside these ranges and needn't reach their ends.
All inputs are finite; a program needn't handle non-finite values.
Results may differ from the reference program's by a relative error of at most 0.0095.
Values may be sent and summed in bfloat16 or wider, within the bound.
A program may use at most 64 MiB of HBM per device.

```python
import math
import jax
import jax.numpy as jnp
from jax import lax

D = 6656
VOCAB = 128
FRAGS = 52
FRAG_COLS = 128
TOK_DEV = 512
TOKENS = 4096
ISLANDS = 4
N_FSDP = 8


def draw_params(key, part):
    key = jax.random.fold_in(key, 7)
    row_key, col_key, base_key = jax.random.split(key, 3)
    row_scale = jnp.exp(jax.random.uniform(row_key, (ISLANDS, VOCAB, 2, 1), jnp.float32, -1.15, 1.15))
    col_scale = jnp.exp(jax.random.uniform(col_key, (ISLANDS, 1, 2, D), jnp.float32, -1.15, 1.15))
    values = jnp.clip(jax.random.normal(base_key, (ISLANDS, VOCAB, 2, D), jnp.float32), -4.0, 4.0) * row_scale * col_scale
    return values


def plant(drawn, own_key, low, largest):
    index_at = [jax.random.randint(jax.random.fold_in(own_key, axis), (), 0, length) for axis, length in enumerate(drawn.shape)]
    longest = drawn.shape.index(max(drawn.shape))
    beside = index_at[:longest] + [(index_at[longest] + 1) % drawn.shape[longest]] + index_at[longest + 1:]
    return drawn.at[tuple(index_at)].set(low).at[tuple(beside)].set(largest)


def shard_levels(stream_key, dims, shards, smallest, high):
    level, own = 1.0, jax.random.fold_in(stream_key, 6)
    for axis_at, parts in shards:
        steps = jnp.exp(jax.random.uniform(jax.random.fold_in(own, axis_at), (parts,), jnp.float32, smallest / len(shards), high / len(shards)))
        level = level * jnp.repeat(steps, dims[axis_at] // parts).reshape([-1 if axis == axis_at else 1 for axis in range(len(dims))])
    return level


def normal_values(rng, dims, deviation, bound, cuts=(), kind=jnp.bfloat16):
    result = jax.random.normal(rng, dims, jnp.float32) * deviation
    if len(cuts) > 0:
        result = shard_levels(rng, dims, cuts, -0.22, 0.18) * result
    return jnp.clip(result, min=-bound, max=bound).astype(kind)


def setup_inputs(seed: int = 0) -> dict:
    key_of = jax.random.split(jax.random.key(seed), 9)
    params = draw_params(jax.random.fold_in(key_of[8], 71), 0)
    adam_m = normal_values(key_of[1], (ISLANDS, VOCAB, 2, D), 0.5, 3.0, ((0, 4), (1, 8)), jnp.float32)
    adam_v = jnp.clip(jnp.exp(math.log(4.0) - 3.6888794 * jax.random.uniform(key_of[2], (ISLANDS, VOCAB, 2, D), jnp.float32) ** shard_levels(key_of[2], (ISLANDS, VOCAB, 2, D), ((0, 4), (1, 8)), -0.2, 0.2)), 0.1, 4.0)
    outer_params = normal_values(key_of[3], (VOCAB, 2, D), 1.0, 6.0, ((0, 8),), jnp.float32)
    outer_mom = normal_values(key_of[4], (VOCAB, 2, D), 0.5, 3.0, ((0, 8),), jnp.float32)
    obs_ids = plant(jax.random.randint(key_of[5], (ISLANDS, TOKENS), 0, VOCAB), jax.random.fold_in(key_of[5], 1), 0, VOCAB - 1).astype(jnp.int32)
    act_ids = plant(jax.random.randint(key_of[6], (ISLANDS, TOKENS), 0, VOCAB), jax.random.fold_in(key_of[6], 1), 0, VOCAB - 1).astype(jnp.int32)
    fragment = jax.random.randint(key_of[7], (1,), 0, FRAGS).astype(jnp.int32)
    return dict(params=params, adam_m=adam_m, adam_v=adam_v, outer_params=outer_params, outer_mom=outer_mom, obs_ids=obs_ids, act_ids=act_ids, fragment=fragment)


beta_first = 0.8
beta_second = 0.95
inner_rate = 0.05
decay_rate = 0.1
adam_eps = 1e-08
outer_rate = 0.7
outer_beta = 0.9
mix_weight = 0.5
norm_eps = 1e-06

def device_partial(tables_b, obs_rows, act_rows, logit_scale):
    embed_rows = tables_b[:, 0, :]
    head_rows = tables_b[:, 1, :]
    embedded = jnp.take(embed_rows, obs_rows, axis=0).astype(jnp.float32)
    inv_rms = lax.rsqrt(lax.optimization_barrier(jnp.mean(embedded * embedded, axis=-1, keepdims=True)) + norm_eps)
    normed = (embedded * inv_rms).astype(jnp.bfloat16)
    logits = jnp.dot(normed, head_rows.T, preferred_element_type=jnp.float32) * logit_scale
    probs = jax.nn.softmax(logits, axis=-1)
    target_hot = jax.nn.one_hot(act_rows, VOCAB, dtype=jnp.float32)
    dlogits = (probs - target_hot).astype(jnp.bfloat16)
    head_part = jnp.dot(dlogits.T, normed, preferred_element_type=jnp.float32) * logit_scale
    dnormed = jnp.dot(dlogits, head_rows, preferred_element_type=jnp.float32) * logit_scale
    unit_rows = embedded * inv_rms
    dembedded = (inv_rms * (dnormed - unit_rows * lax.optimization_barrier(jnp.mean(dnormed * unit_rows, axis=-1, keepdims=True)))).astype(jnp.bfloat16)
    embed_part = jax.ops.segment_sum(dembedded.astype(jnp.float32), obs_rows, num_segments=VOCAB)
    return jnp.stack([embed_part, head_part], axis=1).astype(jnp.bfloat16)

def reference(params, adam_m, adam_v, outer_params, outer_mom, obs_ids, act_ids, fragment):
    logit_scale = 2.0 / math.sqrt(D)

    def island_step(island_item):
        tables, moment, second, obs_rows, act_rows = island_item
        tables_b = tables.astype(jnp.bfloat16)
        blocks = (obs_rows.reshape(N_FSDP, TOK_DEV), act_rows.reshape(N_FSDP, TOK_DEV))

        def block_step(block_ids):
            return device_partial(tables_b, block_ids[0], block_ids[1], logit_scale)
        partials = lax.map(block_step, blocks)
        gradient = lax.optimization_barrier(jnp.sum(partials.astype(jnp.float32), axis=0))
        moment_next = beta_first * moment + (1.0 - beta_first) * gradient
        second_next = beta_second * second + (1.0 - beta_second) * gradient * gradient
        stepped = tables - inner_rate * (moment_next / (jnp.sqrt(second_next) + adam_eps) + decay_rate * tables)
        return (stepped, moment_next, second_next)
    stepped, new_moment, new_second = lax.map(island_step, (params, adam_m, adam_v, obs_ids, act_ids))
    offset = (fragment[0] * FRAG_COLS).astype(jnp.int32)
    outer_slice = lax.dynamic_slice_in_dim(outer_params, offset, FRAG_COLS, 2)
    mom_slice = lax.dynamic_slice_in_dim(outer_mom, offset, FRAG_COLS, 2)
    local_slice = lax.dynamic_slice_in_dim(params, offset, FRAG_COLS, 3)
    mean_drift = lax.optimization_barrier(jnp.sum(outer_slice[None] - local_slice, axis=0)) / ISLANDS
    new_mom_slice = outer_beta * mom_slice + mean_drift
    new_outer_slice = outer_slice - outer_rate * (mean_drift + outer_beta * new_mom_slice)
    new_outer_mom = lax.dynamic_update_slice_in_dim(outer_mom, new_mom_slice, offset, 2)
    new_outer = lax.dynamic_update_slice_in_dim(outer_params, new_outer_slice, offset, 2)
    stepped_slice = lax.dynamic_slice_in_dim(stepped, offset, FRAG_COLS, 3)
    merged = mix_weight * stepped_slice + (1.0 - mix_weight) * new_outer_slice[None]
    new_params = lax.dynamic_update_slice_in_dim(stepped, merged, offset, 3)
    return (new_params, new_moment, new_second, new_outer, new_outer_mom)
```

```python
import functools
import math

import jax
import jax.numpy as jnp
from jax import lax
from jax.experimental import pallas as pl
from jax.experimental.pallas import tpu as pltpu
from jax.sharding import PartitionSpec as P

FRAG_COLS = 128
MESH = pl.DeviceIdType.MESH


beta_first = 0.8
beta_second = 0.95
inner_rate = 0.05
decay_rate = 0.1
adam_eps = 1e-08
outer_rate = 0.7
outer_beta = 0.9
mix_weight = 0.5
norm_eps = 1e-06


def dot_nt(a, b):
    return lax.dot_general(a, b, (((1,), (1,)), ((), ())), preferred_element_type=jnp.float32)


def dot_two(a, b):
    high = a.astype(jnp.bfloat16)
    low = (a - high.astype(jnp.float32)).astype(jnp.bfloat16)
    return jnp.dot(high, b, preferred_element_type=jnp.float32) + jnp.dot(
        low, b, preferred_element_type=jnp.float32
    )


def exchange_kernel(
    n, islands, blocks, width,
    tb_ref, obs_ref, act_ref, drift_ref, grad_ref, mean_ref,
    cols, count_mine, count_in, part_mine, part_in, coef_mine, coef_in,
    out_cols, grad_in, drift_in, send_sem, recv_sem, drift_send, drift_recv,
):
    me = lax.axis_index("fsdp")
    isl = lax.axis_index("island")
    rows, model_width = tb_ref.shape[1], tb_ref.shape[2]
    vocab = rows * n
    span = width * FRAG_COLS
    scale = 2.0 / math.sqrt(model_width)

    def start_of(device):
        return (blocks * device) // n

    def window(device):
        return pl.ds(pl.multiple_of(start_of(device) * FRAG_COLS, FRAG_COLS), span)

    def rows_of(device):
        return pl.ds(pl.multiple_of(device * rows, rows), rows)

    peers = [lax.rem(me + k, n) for k in range(n)]

    barrier = pltpu.get_barrier_semaphore()
    for k in range(1, n):
        pl.semaphore_signal(barrier, inc=1, device_id={"fsdp": peers[k]}, device_id_type=MESH)
    for k in range(1, islands):
        pl.semaphore_signal(
            barrier, inc=1, device_id={"island": lax.rem(isl + k, islands)}, device_id_type=MESH
        )
    pl.semaphore_wait(barrier, n - 1 + islands - 1)

    def send(phase, k, src, dst):
        copy = pltpu.make_async_remote_copy(
            src_ref=src, dst_ref=dst,
            send_sem=send_sem.at[phase, k], recv_sem=recv_sem.at[phase, k],
            device_id={"fsdp": peers[k]}, device_id_type=MESH,
        )
        copy.start()
        return copy

    order = list(range(1, n))
    first = [
        send(0, k, tb_ref.at[:, :, window(peers[k])], cols.at[:, rows_of(me), :]) for k in order
    ]
    drifts = []
    for k in range(1, islands):
        copy = pltpu.make_async_remote_copy(
            src_ref=drift_ref, dst_ref=drift_in.at[k],
            send_sem=drift_send.at[k], recv_sem=drift_recv.at[k],
            device_id={"island": lax.rem(isl + k, islands)}, device_id_type=MESH,
        )
        copy.start()
        drifts.append(copy)

    tokens = obs_ref.shape[1]
    ids = lax.broadcasted_iota(jnp.int32, (vocab, tokens), 0)
    obs_hot = (ids == obs_ref[...]).astype(jnp.float32).astype(jnp.bfloat16)
    act_hot = (ids == act_ref[...]).astype(jnp.float32).astype(jnp.bfloat16)
    count_mine[...] = dot_nt(obs_hot, act_hot)
    second = [send(1, k, count_mine.at[rows_of(peers[k])], count_in.at[k]) for k in order]

    cols[:, rows_of(me), :] = tb_ref[:, :, window(me)]
    mine = tb_ref[0].astype(jnp.float32)
    inv_rms = lax.rsqrt(
        jnp.sum(mine * mine, axis=-1, keepdims=True) * (1.0 / model_width) + norm_eps
    )

    for copy in first:
        copy.wait_recv()
    own_cols = (start_of(me + 1) - start_of(me)) * FRAG_COLS
    embed = cols[0]
    head = cols[1]
    kept = lax.broadcasted_iota(jnp.int32, (vocab, span), 1) < own_cols
    counted = jnp.where(kept, embed.astype(jnp.float32), 0.0).astype(jnp.bfloat16)
    part_mine[...] = dot_nt(counted, head)
    third = [send(2, k, part_mine.at[rows_of(peers[k])], part_in.at[k]) for k in order]

    for copy in second:
        copy.wait_recv()
    counts = count_mine[rows_of(me), :]
    for k in order:
        counts += count_in[k]
    for copy in third:
        copy.wait_recv()
    products = part_mine[rows_of(me), :]
    for k in order:
        products += part_in[k]
    logits = products * inv_rms * scale
    expon = jnp.exp(logits - jnp.max(logits, axis=-1, keepdims=True))
    probs = expon / jnp.sum(expon, axis=-1, keepdims=True)
    missed = probs.astype(jnp.bfloat16).astype(jnp.float32)
    target = (probs - 1.0).astype(jnp.bfloat16).astype(jnp.float32)
    total = jnp.sum(counts, axis=-1, keepdims=True)
    dlogits = (total - counts) * missed + counts * target
    slope = jnp.sum(dlogits * logits, axis=-1, keepdims=True) * (1.0 / model_width)
    shrink = inv_rms * inv_rms * slope
    coef_mine[0:rows, :] = dlogits * (inv_rms * scale)
    here = lax.broadcasted_iota(jnp.int32, (rows, vocab), 0) + me * rows
    lane = lax.broadcasted_iota(jnp.int32, (rows, vocab), 1)
    shrink_row = jnp.sum(jnp.where(here == lane, shrink, 0.0), axis=0, keepdims=True)
    coef_mine[rows:, :] = jnp.broadcast_to(shrink_row, (coef_mine.shape[0] - rows, vocab))
    fourth = [send(3, k, coef_mine, coef_in.at[me]) for k in order]
    coef_in[me] = coef_mine[...]

    for copy in drifts:
        copy.wait_recv()
    drift = drift_ref[...]
    for k in range(1, islands):
        drift += drift_in[k]
    mean_ref[...] = drift * (1.0 / islands)

    for copy in fourth:
        copy.wait_recv()
    coef = jnp.concatenate([coef_in[d, 0:rows, :] for d in range(n)], axis=0)
    shrinks = coef_in[0, rows : rows + 1, :]
    for d in range(1, n):
        shrinks += coef_in[d, rows : rows + 1, :]
    across = lax.broadcasted_iota(jnp.int32, (vocab, vocab), 0)
    down = lax.broadcasted_iota(jnp.int32, (vocab, vocab), 1)
    shrink_col = jnp.sum(jnp.where(across == down, shrinks, 0.0), axis=1, keepdims=True)
    embed_grad = dot_two(coef, head) - shrink_col * embed.astype(jnp.float32)
    out_cols[0] = embed_grad.astype(jnp.bfloat16)
    out_cols[1] = dot_two(coef.T, embed).astype(jnp.bfloat16)
    fifth = [send(4, k, out_cols.at[:, rows_of(peers[k]), :], grad_in.at[me]) for k in order]
    grad_in[me] = out_cols[:, rows_of(me), :]

    for copy in fifth:
        copy.wait_recv()
    for d in range(n):
        at = start_of(d) * FRAG_COLS
        size = (start_of(d + 1) - start_of(d)) * FRAG_COLS
        grad_ref[:, :, at : at + size] = grad_in[d, :, :, 0:size]
    for copy in first + second + third + fourth + fifth + drifts:
        copy.wait_send()


def exchange(tables_b, obs_ids, act_ids, drifts):
    n = lax.axis_size("fsdp")
    islands = lax.axis_size("island")
    rows, model_width = tables_b.shape[1], tables_b.shape[2]
    vocab = rows * n
    blocks = model_width // FRAG_COLS
    width = -(-blocks // n)
    span = width * FRAG_COLS
    vmem = pl.BlockSpec(memory_space=pltpu.VMEM)
    return pl.pallas_call(
        functools.partial(exchange_kernel, n, islands, blocks, width),
        out_shape=(
            jax.ShapeDtypeStruct(tables_b.shape, jnp.bfloat16),
            jax.ShapeDtypeStruct(drifts.shape, jnp.float32),
        ),
        in_specs=[vmem] * 4,
        out_specs=(vmem, vmem),
        scratch_shapes=[
            pltpu.VMEM((2, vocab, span), jnp.bfloat16),
            pltpu.VMEM((vocab, vocab), jnp.float32),
            pltpu.VMEM((n, rows, vocab), jnp.float32),
            pltpu.VMEM((vocab, vocab), jnp.float32),
            pltpu.VMEM((n, rows, vocab), jnp.float32),
            pltpu.VMEM((rows + 8, vocab), jnp.float32),
            pltpu.VMEM((n, rows + 8, vocab), jnp.float32),
            pltpu.VMEM((2, vocab, span), jnp.bfloat16),
            pltpu.VMEM((n, 2, rows, span), jnp.bfloat16),
            pltpu.VMEM((islands,) + drifts.shape, jnp.float32),
            pltpu.SemaphoreType.DMA((5, n)),
            pltpu.SemaphoreType.DMA((5, n)),
            pltpu.SemaphoreType.DMA((islands,)),
            pltpu.SemaphoreType.DMA((islands,)),
        ],
        compiler_params=pltpu.CompilerParams(
            collective_id=0, has_side_effects=True, vmem_limit_bytes=24 * 1024 * 1024
        ),
        cost_estimate=pl.CostEstimate(
            flops=10 * vocab * vocab * span, bytes_accessed=3 * tables_b.size * 2,
            transcendentals=rows * vocab,
        ),
    )(tables_b, obs_ids, act_ids, drifts)


def gathered_gradient(tables_b, obs_ids, act_ids):
    n = lax.axis_size("fsdp")
    rows, model_width = tables_b.shape[1], tables_b.shape[2]
    vocab = rows * n
    scale = 2.0 / math.sqrt(model_width)
    ids = lax.broadcasted_iota(jnp.int32, (vocab, obs_ids.shape[1]), 0)
    obs_hot = (ids == obs_ids).astype(jnp.bfloat16)
    act_hot = (ids == act_ids).astype(jnp.bfloat16)
    counts = lax.psum(dot_nt(obs_hot, act_hot), "fsdp")
    gathered = lax.all_gather(tables_b, "fsdp", axis=1, tiled=True)
    embed, head = gathered[0], gathered[1]
    wide = embed.astype(jnp.float32)
    inv_rms = lax.rsqrt(jnp.mean(wide * wide, axis=-1, keepdims=True) + norm_eps)
    logits = dot_nt(embed, head) * inv_rms * scale
    probs = jax.nn.softmax(logits, axis=-1)
    missed = probs.astype(jnp.bfloat16).astype(jnp.float32)
    target = (probs - 1.0).astype(jnp.bfloat16).astype(jnp.float32)
    total = jnp.sum(counts, axis=-1, keepdims=True)
    dlogits = (total - counts) * missed + counts * target
    slope = jnp.mean(dlogits * logits, axis=-1, keepdims=True) * (vocab / model_width)
    coef = dlogits * (inv_rms * scale)
    shrink = inv_rms * inv_rms * slope
    at = lax.axis_index("fsdp") * rows
    mine = lambda x, axis: lax.dynamic_slice_in_dim(x, at, rows, axis)
    embed_grad = dot_two(mine(coef, 0), head) - mine(shrink, 0) * mine(wide, 0)
    head_grad = dot_two(mine(coef, 1).T, embed)
    return jnp.stack([embed_grad, head_grad])


def on_device(params, adam_m, adam_v, outer_params, outer_mom, obs_ids, act_ids, fragment):
    tables = params[0]
    tables_b = jnp.swapaxes(tables.astype(jnp.bfloat16), 0, 1)
    islands = lax.axis_size("island")
    offset = fragment[0] * FRAG_COLS
    outer_slice = lax.dynamic_slice_in_dim(outer_params, offset, FRAG_COLS, 2)
    mom_slice = lax.dynamic_slice_in_dim(outer_mom, offset, FRAG_COLS, 2)
    drifts = outer_slice - lax.dynamic_slice_in_dim(tables, offset, FRAG_COLS, 2)
    if tables.shape[0] % 16 == 0:
        gradient, mean_drift = exchange(tables_b, obs_ids, act_ids, jnp.swapaxes(drifts, 0, 1))
        mean_drift = jnp.swapaxes(mean_drift, 0, 1)
    else:
        gradient = gathered_gradient(tables_b, obs_ids, act_ids)
        mean_drift = lax.psum(drifts, "island") / islands
    gradient = jnp.swapaxes(gradient, 0, 1).astype(jnp.float32)
    new_mom_slice = outer_beta * mom_slice + mean_drift
    new_outer_slice = outer_slice - outer_rate * (mean_drift + outer_beta * new_mom_slice)
    new_moment = beta_first * adam_m[0] + (1.0 - beta_first) * gradient
    new_second = beta_second * adam_v[0] + (1.0 - beta_second) * gradient * gradient
    stepped = tables - inner_rate * (
        new_moment / (jnp.sqrt(new_second) + adam_eps) + decay_rate * tables
    )
    stepped_slice = lax.dynamic_slice_in_dim(stepped, offset, FRAG_COLS, 2)
    merged = mix_weight * stepped_slice + (1.0 - mix_weight) * new_outer_slice
    new_params = lax.dynamic_update_slice_in_dim(stepped, merged, offset, 2)
    new_outer = lax.dynamic_update_slice_in_dim(outer_params, new_outer_slice, offset, 2)
    new_outer_mom = lax.dynamic_update_slice_in_dim(outer_mom, new_mom_slice, offset, 2)
    return (new_params[None], new_moment[None], new_second[None], new_outer, new_outer_mom)


def solution(mesh):
    in_specs = (
        P("island", "fsdp", None, None),
        P("island", "fsdp", None, None),
        P("island", "fsdp", None, None),
        P("fsdp", None, None),
        P("fsdp", None, None),
        P("island", "fsdp"),
        P("island", "fsdp"),
        P(),
    )
    out_specs = (
        P("island", "fsdp", None, None),
        P("island", "fsdp", None, None),
        P("island", "fsdp", None, None),
        P("fsdp", None, None),
        P("fsdp", None, None),
    )
    return jax.shard_map(
        on_device, mesh=mesh, in_specs=in_specs, out_specs=out_specs, check_vma=False
    )
```
